512 devices in a mesh: dp: 16 (over x, z_hi, core), seq: 32 (over y, z_lo).
Axes of the slice: x: 4, y: 8, z: 8 (z_hi: 2, z_lo: 4; z = z_hi * 4 + z_lo), core: 2. Of those that a mesh axis runs over, the one named last changes fastest.
Arguments:
- queries: bfloat16 [4096, 32, 128], P('seq', 'dp'), may hold values from -14 to 14
- keys: bfloat16 [4096, 32, 128], P('seq', 'dp'), may hold values from -14 to 14
- values: bfloat16 [4096, 32, 128], P('seq', 'dp'), may hold values from -6 to 6
- tan_queries: bfloat16 [4096, 32, 128], P('seq', 'dp'), may hold values from -6 to 6
- tan_keys: bfloat16 [4096, 32, 128], P('seq', 'dp'), may hold values from -6 to 6
- tan_values: bfloat16 [4096, 32, 128], P('seq', 'dp'), may hold values from -6 to 6
- gain_q: float32 [4096], P('dp'), may hold values from 0.7 to 2.5
- gain_k: float32 [4096], P('dp'), may hold values from 0.7 to 2.5
Outputs:
- primal_out: bfloat16 [4096, 32, 128], P('seq', 'dp')
- tangent_out: bfloat16 [4096, 32, 128], P('seq', 'dp')
The draws below stay inside these ranges and needn't reach their ends.
All inputs are finite; a program needn't handle non-finite values.
Results may differ from the reference program's by a relative error of at most 0.012.
Values may be sent and summed in bfloat16 or wider, within the bound.
No kernel may reach another device: no remote copies, remote signals or barrier semaphores. Data moves between devices by JAX's collectives and lax.ppermute only.
A program may use at most 64 MiB of HBM per device.

```python
import math
import jax
import jax.numpy as jnp
from jax import lax

HS = 128
HEADS = 32
LENGTH = 4096


def shared_base(key):
    shape = (LENGTH, HEADS, HS)
    gaussian = jnp.clip(jax.random.normal(key, shape, jnp.float32), -4.0, 4.0)
    rising = 1.0 + 0.75 * jnp.arange(HEADS, dtype=jnp.float32) / max(HEADS - 1, 1)
    return gaussian * rising[None, :, None]


def draw_keys(key, part):
    return shared_base(key).astype(jnp.bfloat16)


def draw_queries(key, part):
    key = jax.random.fold_in(key, 5)
    return shared_base(key).astype(jnp.bfloat16)


def level_of(own_key, shape, cuts, smallest, high):
    loudness = 1.0
    for dim, blocks in cuts:
        heights = jax.random.uniform(jax.random.fold_in(jax.random.fold_in(own_key, 6), dim), (blocks,), jnp.float32, smallest / len(cuts), high / len(cuts))
        loudness = loudness * jnp.repeat(jnp.exp(heights), shape[dim] // blocks).reshape((-1,) + (1,) * (len(shape) - 1 - dim))
    return loudness


def scatter_about(rng, dims, scale, reach, shards=(), kind=jnp.bfloat16):
    values = scale * jax.random.normal(rng, dims, jnp.float32)
    if shards:
        values = values * level_of(rng, dims, shards, -0.22, 0.18)
    return jnp.clip(values, -reach, reach).astype(kind)


def setup_inputs(seed: int = 0) -> dict:
    seeds = jax.random.split(jax.random.key(seed), 9)
    queries = draw_queries(jax.random.fold_in(seeds[8], 71), 0)
    keys = draw_keys(jax.random.fold_in(seeds[8], 71), 0)
    values = scatter_about(seeds[2], (LENGTH, HEADS, HS), 1.0, 6.0, ((0, 32), (1, 16)))
    tan_queries = scatter_about(seeds[3], (LENGTH, HEADS, HS), 1.0, 6.0, ((0, 32), (1, 16)))
    tan_keys = scatter_about(seeds[4], (LENGTH, HEADS, HS), 1.0, 6.0, ((0, 32), (1, 16)))
    tan_values = scatter_about(seeds[5], (LENGTH, HEADS, HS), 1.0, 6.0, ((0, 32), (1, 16)))
    gain_q = jnp.clip(jnp.exp(math.log(2.5) - 1.2729657 * jax.random.uniform(seeds[6], (HEADS * HS,), jnp.float32) ** level_of(seeds[6], (HEADS * HS,), ((0, 16),), -0.2, 0.2)), 0.7, 2.5)
    gain_k = jnp.clip(jnp.exp(math.log(2.5) - 1.2729657 * jax.random.uniform(seeds[7], (HEADS * HS,), jnp.float32) ** level_of(seeds[7], (HEADS * HS,), ((0, 16),), -0.2, 0.2)), 0.7, 2.5)
    return {"queries": queries, "keys": keys, "values": values, "tan_queries": tan_queries, "tan_keys": tan_keys, "tan_values": tan_values, "gain_q": gain_q, "gain_k": gain_k}


EPSILON = 1e-06

def norm_pair(primal, tangent, gain):
    mean_square = lax.optimization_barrier(jnp.mean(primal * primal, axis=-1, keepdims=True))
    cross_mean = lax.optimization_barrier(jnp.mean(primal * tangent, axis=-1, keepdims=True))
    inverse = lax.rsqrt(mean_square + EPSILON)
    normed = gain * (primal * inverse)
    tan_normed = gain * (tangent * inverse - primal * (inverse * inverse * inverse) * cross_mean)
    return (normed.astype(jnp.bfloat16), tan_normed.astype(jnp.bfloat16))

def attend_block(query_block, tan_query_block, key_head, value_head, tan_key_head, tan_value_head):
    factor = query_block.shape[-1] ** (-0.5)
    scores = jnp.dot(query_block, key_head.T, preferred_element_type=jnp.float32) * factor
    tan_scores = (jnp.dot(tan_query_block, key_head.T, preferred_element_type=jnp.float32) + jnp.dot(query_block, tan_key_head.T, preferred_element_type=jnp.float32)) * factor
    row_max = lax.optimization_barrier(jnp.max(scores, axis=-1, keepdims=True))
    shifted = jnp.exp(scores - row_max)
    totals = lax.optimization_barrier(jnp.sum(shifted, axis=-1, keepdims=True))
    weights = shifted / totals
    weights_low = weights.astype(jnp.bfloat16)
    output = jnp.dot(weights_low, value_head, preferred_element_type=jnp.float32).astype(jnp.bfloat16)
    tan_weights = weights * (tan_scores - lax.optimization_barrier(jnp.sum(weights * tan_scores, axis=-1, keepdims=True)))
    tan_low = tan_weights.astype(jnp.bfloat16)
    tangent = (jnp.dot(tan_low, value_head, preferred_element_type=jnp.float32) + jnp.dot(weights_low, tan_value_head, preferred_element_type=jnp.float32)).astype(jnp.bfloat16)
    return (output, tangent)

def attend_head(members):
    query_head, key_head, value_head, tan_query_head, tan_key_head, tan_value_head = members
    total_rows = query_head.shape[0]
    block_rows = math.gcd(total_rows, 512)
    count_blocks = total_rows // block_rows
    query_blocks = query_head.reshape(count_blocks, block_rows, query_head.shape[-1])
    tan_blocks = tan_query_head.reshape(count_blocks, block_rows, query_head.shape[-1])

    def one_block(pieces):
        return attend_block(pieces[0], pieces[1], key_head, value_head, tan_key_head, tan_value_head)
    output, tangent = lax.map(one_block, (query_blocks, tan_blocks))
    return (output.reshape(total_rows, -1), tangent.reshape(total_rows, -1))

def reference(queries, keys, values, tan_queries, tan_keys, tan_values, gain_q, gain_k):
    feature_count = HEADS * HS

    def head_major(array):
        return array.reshape(LENGTH, HEADS, HS).transpose(1, 0, 2)
    normed_q, normed_tq = norm_pair(queries.reshape(LENGTH, feature_count).astype(jnp.float32), tan_queries.reshape(LENGTH, feature_count).astype(jnp.float32), gain_q)
    normed_k, normed_tk = norm_pair(keys.reshape(LENGTH, feature_count).astype(jnp.float32), tan_keys.reshape(LENGTH, feature_count).astype(jnp.float32), gain_k)
    output, tangent = lax.map(attend_head, (head_major(normed_q), head_major(normed_k), values.transpose(1, 0, 2), head_major(normed_tq), head_major(normed_tk), tan_values.transpose(1, 0, 2)))
    return (output.transpose(1, 0, 2), tangent.transpose(1, 0, 2))
```

```python
import functools
import math

import jax
import jax.numpy as jnp
from jax import lax
from jax.experimental import pallas as pl
from jax.experimental.pallas import tpu as pltpu
from jax.sharding import PartitionSpec as P

HS = 128
HEADS = 32
FEATURES = HEADS * HS
EPSILON = 1e-06
FACTOR = HS**-0.5
LOG2E = math.log2(math.e)

Y, Z, DP = 8, 4, 16
ROWS = 128
LOCAL = 2
PART = 528

Z_GROUPS = [[y * Z + z for z in range(Z)] for y in range(Y)]
Y_GROUPS = [[y * Z + z for y in range(Y)] for z in range(Z)]

VMEM_LIMIT = 40 * 1024 * 1024
VMEM_WHOLE = 60 * 1024 * 1024
SMALL = pl.CostEstimate(flops=1, bytes_accessed=1, transcendentals=0)


def params(limit=VMEM_LIMIT):
    return pltpu.CompilerParams(vmem_limit_bytes=limit)


def swaps(size, bits):
    return [(i, i ^ bits) for i in range(size)]


def loader(refs, raw, wide, sems):
    loads = [pltpu.make_async_copy(ref, raw.at[i], sems.at[i]) for i, ref in enumerate(refs)]
    for load in loads:
        load.start()

    def heads(i):
        loads[i].wait()
        wide[i] = raw[i].astype(jnp.float32)
        return [wide[i, pl.ds(h, ROWS, stride=LOCAL), :] for h in range(LOCAL)]

    return heads


def stats_kernel(q, k, tq, tk, gain_q, gain_k, stat_out, scaled_out, raw, wide, gains, sems):
    gain_loads = [
        pltpu.make_async_copy(ref, gains.at[i], sems.at[4 + i])
        for i, ref in enumerate((gain_q, gain_k))
    ]
    for load in gain_loads:
        load.start()
    heads = loader((q, tq, k, tk), raw, wide, sems)
    pairs = [heads(i) for i in range(4)]
    for load in gain_loads:
        load.wait()
    rows = []
    for i in (0, 1):
        primal, tangent = pairs[2 * i], pairs[2 * i + 1]
        for other in (primal, tangent):
            product = primal[0] * other[0] + primal[1] * other[1]
            rows.append(jnp.sum(product.T, axis=0, keepdims=True))
        if i == 0:
            for h in range(LOCAL):
                scaled_out[0, h, 0:ROWS] = gains[0, h : h + 1] * primal[h]
                scaled_out[1, h, 0:ROWS] = gains[0, h : h + 1] * tangent[h]
                tail = jnp.broadcast_to(gains[1, h : h + 1], (8, HS))
                scaled_out[0, h, ROWS:] = tail
                scaled_out[1, h, ROWS:] = tail
    stat_out[...] = jnp.broadcast_to(jnp.concatenate(rows, axis=0)[None], stat_out.shape)


def split_three(x):
    high = x.astype(jnp.bfloat16).astype(jnp.float32)
    rest = x - high
    middle = rest.astype(jnp.bfloat16).astype(jnp.float32)
    return [high, middle, rest - middle]


def bulk_kernel(k, tk, v, tv, out, raw, wide, packed, sems):
    heads = loader((k, tk, v, tv), raw, wide, sems)
    for i in range(4):
        for h, block in enumerate(heads(i)):
            block = block if i < 2 else block.T
            packed[h, i * 128 : (i + 1) * 128] = block.astype(jnp.bfloat16)
    send = pltpu.make_async_copy(packed, out, sems.at[4])
    send.start()
    send.wait()


def inverse_and_cross(squares, crosses):
    inverse = lax.rsqrt(squares * (1.0 / FEATURES) + EPSILON)
    cross = inverse * inverse * inverse * (crosses * (1.0 / FEATURES))
    return [jnp.broadcast_to(row, (ROWS, ROWS)).T for row in (inverse, cross)]


def norm_kernel(parts, scaled, q_out, key_out, gain_out):
    bf16 = jnp.bfloat16
    stats = jnp.sum(parts[...], axis=0)
    inverse, cross = inverse_and_cross(stats[0:1], stats[1:2])
    for h in range(LOCAL):
        primal, tangent = scaled[0, h, 0:ROWS], scaled[1, h, 0:ROWS]
        gain_out[h] = scaled[0, h, ROWS:]
        q_out[h, 0:128] = (primal * inverse).astype(bf16)
        q_out[h, 128:256] = (tangent * inverse - primal * cross).astype(bf16)
    key_out[...] = jnp.broadcast_to(stats[2:4][None], key_out.shape)


def stack_rows(rows, cols):
    index = lax.broadcasted_iota(jnp.int32, (16, cols), 0)
    tile = jnp.zeros((16, cols), jnp.float32)
    for i, row in enumerate(rows):
        tile = jnp.where(index == i, row, tile)
    return tile.astype(jnp.bfloat16)


def coef_kernel(sums, gains, coef):
    for y in range(Y):
        inverse, cross = inverse_and_cross(sums[y, 0:1], sums[y, 1:2])
        for h in range(LOCAL):
            coef[0, y, h] = inverse * gains[h, 0:1]
            coef[1, y, h] = cross * gains[h, 0:1]


def attend_kernel(count, bulk, normed, *refs):
    f32, bf16 = jnp.float32, jnp.bfloat16
    queries, outs, (s_ref, t_ref) = refs[:count], refs[count : 2 * count], refs[-2:]
    if count > 1:
        coef, normed = normed, refs[2 * count]
        for h in range(LOCAL):
            for y in range(Y):
                key = bulk[y, h, 0:128].astype(f32)
                tan_key = bulk[y, h, 128:256].astype(f32)
                normed[y, h, 0:128] = (key * coef[0, y, h]).astype(bf16)
                normed[y, h, 128:256] = (tan_key * coef[0, y, h] - key * coef[1, y, h]).astype(bf16)
    nt = (((1,), (1,)), ((), ()))
    cols = count * ROWS

    rows = []
    for h in range(LOCAL):
        query = jnp.concatenate([q[h, 0:128] for q in queries], axis=0)
        tan_query = jnp.concatenate([q[h, 128:256] for q in queries], axis=0)
        both = jnp.concatenate([tan_query, query], axis=1)
        high = None
        for start in range(0, Y, 4):
            key = jnp.concatenate([normed[y, h, 0:128] for y in range(start, start + 4)], axis=0)
            score = lax.dot_general(key, query, nt, preferred_element_type=f32)
            for i, y in enumerate(range(start, start + 4)):
                scaled = score[i * 128 : (i + 1) * 128] * (FACTOR * LOG2E)
                s_ref[y] = scaled
                block_high = jnp.max(scaled.reshape(16, 8, cols), axis=0)
                high = block_high if high is None else jnp.maximum(high, block_high)
        high = jnp.max(high, axis=0, keepdims=True)
        total = jnp.zeros((8, cols), f32)
        cross = jnp.zeros((8, cols), f32)
        out = jnp.zeros((HS, cols), f32)
        tangent = jnp.zeros((HS, cols), f32)
        for start in range(0, Y, 2):
            pair = range(start, start + 2)
            keys = jnp.concatenate(
                [
                    jnp.concatenate([normed[y, h, first : first + 128] for y in pair], axis=0)
                    for first in (0, 128)
                ],
                axis=1,
            )
            tan = lax.dot_general(keys, both, nt, preferred_element_type=f32)
            lows = []
            for i, y in enumerate(pair):
                scaled = s_ref[y]
                weight = jnp.exp2(scaled - high)
                tan_score = tan[i * 128 : (i + 1) * 128] * FACTOR
                s_ref[y] = weight
                t_ref[y] = tan_score
                total = total + jnp.sum(weight.reshape(16, 8, cols), axis=0)
                cross = cross + jnp.sum((weight * tan_score).reshape(16, 8, cols), axis=0)
                lows.append(weight.astype(bf16))
            values = jnp.concatenate(
                [
                    jnp.concatenate([bulk[y, h, first : first + 128] for y in pair], axis=1)
                    for first in (256, 384)
                ],
                axis=0,
            )
            sums = jnp.dot(values, jnp.concatenate(lows, axis=0), preferred_element_type=f32)
            out = out + sums[0:128]
            tangent = tangent + sums[128:256]
        total = jnp.sum(total, axis=0, keepdims=True)
        inverse = 1.0 / total
        mean = jnp.sum(cross, axis=0, keepdims=True) * inverse
        for start in range(0, Y, 2):
            pair = range(start, start + 2)
            tan_lows = [(s_ref[y] * (t_ref[y] - mean)).astype(bf16) for y in pair]
            tangent = tangent + jnp.dot(
                jnp.concatenate([bulk[y, h, 256:384] for y in pair], axis=1),
                jnp.concatenate(tan_lows, axis=0),
                preferred_element_type=f32,
            )
        out = (out * inverse).astype(bf16)
        tangent = (tangent * inverse).astype(bf16)
        rows += split_three(high + jnp.log2(total)) + split_three(mean)
        for i, ref in enumerate(outs):
            lanes = slice(i * ROWS, (i + 1) * ROWS)
            ref[h * 256 : h * 256 + 128] = out[:, lanes]
            ref[h * 256 + 128 : h * 256 + 256] = tangent[:, lanes]
    stats = stack_rows(rows, cols)
    for i, ref in enumerate(outs):
        ref[512:PART] = stats[:, i * ROWS : (i + 1) * ROWS]
        if ref.shape[0] > PART:
            ref[PART:] = jnp.zeros((ref.shape[0] - PART, HS), bf16)


def merge_kernel(p0, p1, p2, p3, out_ref, tan_ref, wide):
    f32, bf16 = jnp.float32, jnp.bfloat16
    for h in range(LOCAL):
        parts = (p0, p1, p2, p3)
        logs, means = [], []
        for z in range(Z):
            stats = parts[z][512:528].astype(f32)[6 * h : 6 * h + 6]
            logs.append(stats[0:1] + stats[1:2] + stats[2:3])
            means.append(stats[3:4] + stats[4:5] + stats[5:6])
        top = jnp.maximum(jnp.maximum(logs[0], logs[1]), jnp.maximum(logs[2], logs[3]))
        weights = [jnp.exp2(x - top) for x in logs]
        inverse = 1.0 / (weights[0] + weights[1] + weights[2] + weights[3])
        weights = [w * inverse for w in weights]
        mean = sum(w * m for w, m in zip(weights, means))
        out = jnp.zeros((HS, ROWS), f32)
        tangent = jnp.zeros((HS, ROWS), f32)
        for z in range(Z):
            piece = parts[z][h * 256 : h * 256 + 128].astype(f32)
            out = out + weights[z] * piece
            tangent = tangent + weights[z] * parts[z][h * 256 + 128 : h * 256 + 256].astype(f32)
            tangent = tangent + (weights[z] * (means[z] - mean)) * piece
        wide[0, pl.ds(h, ROWS, stride=LOCAL), :] = out.T
        wide[1, pl.ds(h, ROWS, stride=LOCAL), :] = tangent.T
    out_ref[...] = wide[0].astype(bf16)
    tan_ref[...] = wide[1].astype(bf16)


def shards(queries, keys, values, tan_queries, tan_keys, tan_values, gain_q, gain_k):
    f32, bf16 = jnp.float32, jnp.bfloat16
    flat = lambda x: x.reshape(ROWS * LOCAL, HS)
    q, k, v = flat(queries), flat(keys), flat(values)
    tq, tk, tv = flat(tan_queries), flat(tan_keys), flat(tan_values)
    raw = lambda n: pltpu.VMEM((n, ROWS * LOCAL, HS), bf16)
    wide = lambda n: pltpu.VMEM((n, ROWS * LOCAL, HS), f32)
    hbm = pl.BlockSpec(memory_space=pltpu.HBM)
    vmem = pl.BlockSpec(memory_space=pltpu.VMEM)
    struct = jax.ShapeDtypeStruct
    block = (Y, LOCAL, 256, HS)

    stats, scaled = pl.pallas_call(
        stats_kernel,
        out_shape=(struct((DP, 4, ROWS), f32), struct((2, LOCAL, ROWS + 8, HS), f32)),
        in_specs=[hbm] * 6,
        out_specs=(vmem, vmem),
        scratch_shapes=[
            raw(4),
            wide(4),
            pltpu.VMEM((2, LOCAL, HS), f32),
            pltpu.SemaphoreType.DMA((6,)),
        ],
        compiler_params=params(VMEM_WHOLE),
        cost_estimate=SMALL,
        name="stats",
    )(q, k, tq, tk, gain_q.reshape(LOCAL, HS), gain_k.reshape(LOCAL, HS))
    bulk = pl.pallas_call(
        bulk_kernel,
        out_shape=struct((LOCAL, 512, HS), bf16),
        in_specs=[hbm] * 4,
        out_specs=hbm,
        scratch_shapes=[
            raw(4),
            wide(4),
            pltpu.VMEM((LOCAL, 512, HS), bf16),
            pltpu.SemaphoreType.DMA((5,)),
        ],
        compiler_params=params(VMEM_WHOLE),
        cost_estimate=SMALL,
        name="bulk",
    )(k, tk, v, tv)
    bulk = lax.all_gather(bulk, "seq", axis_index_groups=Y_GROUPS)
    stats = lax.all_to_all(stats, "dp", 0, 0)
    q_mine, sums, gains = pl.pallas_call(
        norm_kernel,
        out_shape=(
            struct((LOCAL, 256, HS), bf16),
            struct((Y, 2, ROWS), f32),
            struct((LOCAL, 8, HS), f32),
        ),
        compiler_params=params(),
        cost_estimate=SMALL,
        name="norm",
    )(stats, scaled)
    sums = lax.all_to_all(sums, "seq", 0, 0, axis_index_groups=Y_GROUPS)
    trade = lambda x, i: lax.ppermute(x, "seq", swaps(Y * Z, i))
    queries_of = [q_mine] + [trade(q_mine, i) for i in (1, 2, 3)]
    coef = pl.pallas_call(
        coef_kernel,
        out_shape=struct((2, Y, LOCAL, ROWS, HS), f32),
        compiler_params=params(),
        cost_estimate=pl.CostEstimate(flops=1_000_000_000, bytes_accessed=1, transcendentals=0),
        name="coef",
    )(sums, gains)

    def attend(bulk, scales, *blocks):
        count = len(blocks)
        spare = 16 if count > 1 else 0
        return pl.pallas_call(
            functools.partial(attend_kernel, count),
            out_shape=(struct((PART + spare, HS), bf16),) * count
            + (struct((Y, LOCAL, 256, HS), bf16),) * (count > 1),
            scratch_shapes=[pltpu.VMEM((Y, ROWS, count * ROWS), f32)] * 2,
            compiler_params=params(),
            cost_estimate=pl.CostEstimate(
                flops=402_653_184 * count, bytes_accessed=4_000_000, transcendentals=262_144 * count
            ),
            name="attend" + "".join(map(str, blocks)),
        )(bulk, scales, *[queries_of[i] for i in blocks])

    part2, part3, normed = attend(bulk, coef, 2, 3)
    bulk, part2, part3 = lax.optimization_barrier((bulk, part2, part3))
    (part1,) = attend(bulk, normed, 1)
    bulk, part1 = lax.optimization_barrier((bulk, part1))
    (part0,) = attend(bulk, normed, 0)
    parts = [part0, trade(part1, 1), trade(part2, 2), trade(part3, 3)]
    out, tangent = pl.pallas_call(
        merge_kernel,
        out_shape=(struct((ROWS * LOCAL, HS), bf16),) * 2,
        scratch_shapes=[wide(2)],
        compiler_params=params(),
        cost_estimate=SMALL,
        name="merge",
    )(*parts)
    shape = queries.shape
    return (out.reshape(shape), tangent.reshape(shape))


def solution(mesh):
    token = P("seq", "dp", None)
    return jax.shard_map(
        shards,
        mesh=mesh,
        in_specs=(token,) * 6 + (P("dp"), P("dp")),
        out_specs=(token, token),
        check_vma=False,
    )
```

```python
import functools
import math

import jax
import jax.numpy as jnp
from jax import lax
from jax.experimental import pallas as pl
from jax.experimental.pallas import tpu as pltpu
from jax.sharding import PartitionSpec as P

HS = 128
HEADS = 32
FEATURES = HEADS * HS
EPSILON = 1e-06
FACTOR = HS**-0.5
LOG2E = math.log2(math.e)

Y, Z, DP = 8, 4, 16
ROWS = 128
LOCAL = 2
PART = 528

Z_GROUPS = [[y * Z + z for z in range(Z)] for y in range(Y)]
Y_GROUPS = [[y * Z + z for y in range(Y)] for z in range(Z)]

VMEM_LIMIT = 40 * 1024 * 1024
VMEM_WHOLE = 60 * 1024 * 1024
SMALL = pl.CostEstimate(flops=1, bytes_accessed=1, transcendentals=0)


def params(limit=VMEM_LIMIT):
    return pltpu.CompilerParams(vmem_limit_bytes=limit)


def swaps(size, bits):
    return [(i, i ^ bits) for i in range(size)]


def loader(refs, raw, wide, sems):
    loads = [pltpu.make_async_copy(ref, raw.at[i], sems.at[i]) for i, ref in enumerate(refs)]
    for load in loads:
        load.start()

    def heads(i):
        loads[i].wait()
        wide[i] = raw[i].astype(jnp.float32)
        return [wide[i, pl.ds(h, ROWS, stride=LOCAL), :] for h in range(LOCAL)]

    return heads


def stats_kernel(q, k, tq, tk, gain_q, gain_k, stat_out, scaled_out, raw, wide, gains, sems):
    gain_loads = [
        pltpu.make_async_copy(ref, gains.at[i], sems.at[4 + i])
        for i, ref in enumerate((gain_q, gain_k))
    ]
    for load in gain_loads:
        load.start()
    heads = loader((q, tq, k, tk), raw, wide, sems)
    pairs = [heads(i) for i in range(4)]
    for load in gain_loads:
        load.wait()
    rows = []
    for i in (0, 1):
        primal, tangent = pairs[2 * i], pairs[2 * i + 1]
        for other in (primal, tangent):
            product = primal[0] * other[0] + primal[1] * other[1]
            rows.append(jnp.sum(product.T, axis=0, keepdims=True))
        if i == 0:
            for h in range(LOCAL):
                scaled_out[0, h, 0:ROWS] = gains[0, h : h + 1] * primal[h]
                scaled_out[1, h, 0:ROWS] = gains[0, h : h + 1] * tangent[h]
                tail = jnp.broadcast_to(gains[1, h : h + 1], (8, HS))
                scaled_out[0, h, ROWS:] = tail
                scaled_out[1, h, ROWS:] = tail
    stat_out[...] = jnp.broadcast_to(jnp.concatenate(rows, axis=0)[None], stat_out.shape)


def split_three(x):
    high = x.astype(jnp.bfloat16).astype(jnp.float32)
    rest = x - high
    middle = rest.astype(jnp.bfloat16).astype(jnp.float32)
    return [high, middle, rest - middle]


def bulk_kernel(k, tk, v, tv, out, raw, wide, packed, sems):
    heads = loader((k, tk, v, tv), raw, wide, sems)
    pairs = [heads(i) for i in range(4)]
    for i, pair in enumerate(pairs):
        for h, block in enumerate(pair):
            block = block if i < 2 else block.T
            packed[h, i * 128 : (i + 1) * 128] = block.astype(jnp.bfloat16)
    send = pltpu.make_async_copy(packed, out, sems.at[4])
    send.start()
    send.wait()


def inverse_and_cross(squares, crosses):
    inverse = lax.rsqrt(squares * (1.0 / FEATURES) + EPSILON)
    cross = inverse * inverse * inverse * (crosses * (1.0 / FEATURES))
    return [jnp.broadcast_to(row, (ROWS, ROWS)).T for row in (inverse, cross)]


def norm_kernel(parts, scaled, q_out, key_out, gain_out):
    bf16 = jnp.bfloat16
    stats = jnp.sum(parts[...], axis=0)
    inverse, cross = inverse_and_cross(stats[0:1], stats[1:2])
    for h in range(LOCAL):
        primal, tangent = scaled[0, h, 0:ROWS], scaled[1, h, 0:ROWS]
        gain_out[h] = scaled[0, h, ROWS:]
        q_out[h, 0:128] = (primal * inverse).astype(bf16)
        q_out[h, 128:256] = (tangent * inverse - primal * cross).astype(bf16)
    key_out[...] = jnp.broadcast_to(stats[2:4][None], key_out.shape)


def stack_rows(rows, cols):
    index = lax.broadcasted_iota(jnp.int32, (16, cols), 0)
    tile = jnp.zeros((16, cols), jnp.float32)
    for i, row in enumerate(rows):
        tile = jnp.where(index == i, row, tile)
    return tile.astype(jnp.bfloat16)


def coef_kernel(sums, gains, coef):
    for y in range(Y):
        inverse, cross = inverse_and_cross(sums[y, 0:1], sums[y, 1:2])
        for h in range(LOCAL):
            coef[0, y, h] = inverse * gains[h, 0:1]
            coef[1, y, h] = cross * gains[h, 0:1]


def attend_kernel(count, bulk, normed, *refs):
    f32, bf16 = jnp.float32, jnp.bfloat16
    queries, outs, (s_ref, t_ref) = refs[:count], refs[count : 2 * count], refs[-2:]
    if count > 1:
        coef, normed = normed, refs[2 * count]
        for h in range(LOCAL):
            for y in range(Y):
                key = bulk[y, h, 0:128].astype(f32)
                tan_key = bulk[y, h, 128:256].astype(f32)
                normed[y, h, 0:128] = (key * coef[0, y, h]).astype(bf16)
                normed[y, h, 128:256] = (tan_key * coef[0, y, h] - key * coef[1, y, h]).astype(bf16)
    nt = (((1,), (1,)), ((), ()))
    cols = count * ROWS

    rows = []
    for h in range(LOCAL):
        query = jnp.concatenate([q[h, 0:128] for q in queries], axis=0)
        tan_query = jnp.concatenate([q[h, 128:256] for q in queries], axis=0)
        both = jnp.concatenate([tan_query, query], axis=1)
        high = None
        for start in range(0, Y, 4):
            key = jnp.concatenate([normed[y, h, 0:128] for y in range(start, start + 4)], axis=0)
            score = lax.dot_general(key, query, nt, preferred_element_type=f32)
            for i, y in enumerate(range(start, start + 4)):
                scaled = score[i * 128 : (i + 1) * 128] * (FACTOR * LOG2E)
                s_ref[y] = scaled
                block_high = jnp.max(scaled.reshape(16, 8, cols), axis=0)
                high = block_high if high is None else jnp.maximum(high, block_high)
        high = jnp.max(high, axis=0, keepdims=True)
        total = jnp.zeros((8, cols), f32)
        cross = jnp.zeros((8, cols), f32)
        out = jnp.zeros((HS, cols), f32)
        tangent = jnp.zeros((HS, cols), f32)
        for start in range(0, Y, 2):
            pair = range(start, start + 2)
            keys = jnp.concatenate(
                [
                    jnp.concatenate([normed[y, h, first : first + 128] for y in pair], axis=0)
                    for first in (0, 128)
                ],
                axis=1,
            )
            tan = lax.dot_general(keys, both, nt, preferred_element_type=f32)
            lows = []
            for i, y in enumerate(pair):
                scaled = s_ref[y]
                weight = jnp.exp2(scaled - high)
                tan_score = tan[i * 128 : (i + 1) * 128] * FACTOR
                s_ref[y] = weight
                t_ref[y] = tan_score
                total = total + jnp.sum(weight.reshape(16, 8, cols), axis=0)
                cross = cross + jnp.sum((weight * tan_score).reshape(16, 8, cols), axis=0)
                lows.append(weight.astype(bf16))
            values = jnp.concatenate(
                [
                    jnp.concatenate([bulk[y, h, first : first + 128] for y in pair], axis=1)
                    for first in (256, 384)
                ],
                axis=0,
            )
            sums = jnp.dot(values, jnp.concatenate(lows, axis=0), preferred_element_type=f32)
            out = out + sums[0:128]
            tangent = tangent + sums[128:256]
        total = jnp.sum(total, axis=0, keepdims=True)
        inverse = 1.0 / total
        mean = jnp.sum(cross, axis=0, keepdims=True) * inverse
        for start in range(0, Y, 2):
            pair = range(start, start + 2)
            tan_lows = [(s_ref[y] * (t_ref[y] - mean)).astype(bf16) for y in pair]
            tangent = tangent + jnp.dot(
                jnp.concatenate([bulk[y, h, 256:384] for y in pair], axis=1),
                jnp.concatenate(tan_lows, axis=0),
                preferred_element_type=f32,
            )
        out = (out * inverse).astype(bf16)
        tangent = (tangent * inverse).astype(bf16)
        rows += split_three(high + jnp.log2(total)) + split_three(mean)
        for i, ref in enumerate(outs):
            lanes = slice(i * ROWS, (i + 1) * ROWS)
            ref[h * 256 : h * 256 + 128] = out[:, lanes]
            ref[h * 256 + 128 : h * 256 + 256] = tangent[:, lanes]
    stats = stack_rows(rows, cols)
    for i, ref in enumerate(outs):
        ref[512:PART] = stats[:, i * ROWS : (i + 1) * ROWS]
        if ref.shape[0] > PART:
            ref[PART:] = jnp.zeros((ref.shape[0] - PART, HS), bf16)


def statistics(part, h):
    rows = part[512:528].astype(jnp.float32)[6 * h : 6 * h + 6]
    return rows[0:1] + rows[1:2] + rows[2:3], rows[3:4] + rows[4:5] + rows[5:6]


def three_kernel(p0, p2, p3, sum_out, stat_out):
    f32 = jnp.float32
    for h in range(LOCAL):
        logs, means = zip(*[statistics(part, h) for part in (p0, p2, p3)])
        top = jnp.maximum(jnp.maximum(logs[0], logs[1]), logs[2])
        weights = [jnp.exp2(x - top) for x in logs]
        total = weights[0] + weights[1] + weights[2]
        inverse = 1.0 / total
        weights = [w * inverse for w in weights]
        mean = sum(w * m for w, m in zip(weights, means))
        out = jnp.zeros((HS, ROWS), f32)
        tangent = jnp.zeros((HS, ROWS), f32)
        for part, weight, own_mean in zip((p0, p2, p3), weights, means):
            piece = part[h * 256 : h * 256 + 128].astype(f32)
            out = out + weight * piece
            tangent = tangent + weight * part[h * 256 + 128 : h * 256 + 256].astype(f32)
            tangent = tangent + (weight * (own_mean - mean)) * piece
        sum_out[h, 0], sum_out[h, 1] = out, tangent
        stat_out[h, 0] = jnp.broadcast_to(top + jnp.log2(total), (8, ROWS))
        stat_out[h, 1] = jnp.broadcast_to(mean, (8, ROWS))


def merge_kernel(sums, stats, last, out_ref, tan_ref, wide):
    f32, bf16 = jnp.float32, jnp.bfloat16
    for h in range(LOCAL):
        log, mean = stats[h, 0, 0:1], stats[h, 1, 0:1]
        last_log, last_mean = statistics(last, h)
        top = jnp.maximum(log, last_log)
        weight, last_weight = jnp.exp2(log - top), jnp.exp2(last_log - top)
        inverse = 1.0 / (weight + last_weight)
        weight, last_weight = weight * inverse, last_weight * inverse
        piece = last[h * 256 : h * 256 + 128].astype(f32)
        tan_piece = last[h * 256 + 128 : h * 256 + 256].astype(f32)
        out = weight * sums[h, 0] + last_weight * piece
        tangent = weight * sums[h, 1] + last_weight * tan_piece
        tangent = tangent + (weight * last_weight * (mean - last_mean)) * (sums[h, 0] - piece)
        wide[0, pl.ds(h, ROWS, stride=LOCAL), :] = out.T
        wide[1, pl.ds(h, ROWS, stride=LOCAL), :] = tangent.T
    out_ref[...] = wide[0].astype(bf16)
    tan_ref[...] = wide[1].astype(bf16)


def shards(queries, keys, values, tan_queries, tan_keys, tan_values, gain_q, gain_k):
    f32, bf16 = jnp.float32, jnp.bfloat16
    flat = lambda x: x.reshape(ROWS * LOCAL, HS)
    q, k, v = flat(queries), flat(keys), flat(values)
    tq, tk, tv = flat(tan_queries), flat(tan_keys), flat(tan_values)
    raw = lambda n: pltpu.VMEM((n, ROWS * LOCAL, HS), bf16)
    wide = lambda n: pltpu.VMEM((n, ROWS * LOCAL, HS), f32)
    hbm = pl.BlockSpec(memory_space=pltpu.HBM)
    vmem = pl.BlockSpec(memory_space=pltpu.VMEM)
    struct = jax.ShapeDtypeStruct
    block = (Y, LOCAL, 256, HS)

    stats, scaled = pl.pallas_call(
        stats_kernel,
        out_shape=(struct((DP, 4, ROWS), f32), struct((2, LOCAL, ROWS + 8, HS), f32)),
        in_specs=[hbm] * 6,
        out_specs=(vmem, vmem),
        scratch_shapes=[
            raw(4),
            wide(4),
            pltpu.VMEM((2, LOCAL, HS), f32),
            pltpu.SemaphoreType.DMA((6,)),
        ],
        compiler_params=params(VMEM_WHOLE),
        cost_estimate=SMALL,
        name="stats",
    )(q, k, tq, tk, gain_q.reshape(LOCAL, HS), gain_k.reshape(LOCAL, HS))
    bulk = pl.pallas_call(
        bulk_kernel,
        out_shape=struct((LOCAL, 512, HS), bf16),
        in_specs=[hbm] * 4,
        out_specs=hbm,
        scratch_shapes=[
            raw(4),
            wide(4),
            pltpu.VMEM((LOCAL, 512, HS), bf16),
            pltpu.SemaphoreType.DMA((5,)),
        ],
        compiler_params=params(VMEM_WHOLE),
        cost_estimate=SMALL,
        name="bulk",
    )(k, tk, v, tv)
    bulk = lax.all_gather(bulk, "seq", axis_index_groups=Y_GROUPS)
    stats = lax.all_to_all(stats, "dp", 0, 0)
    q_mine, sums, gains = pl.pallas_call(
        norm_kernel,
        out_shape=(
            struct((LOCAL, 256, HS), bf16),
            struct((Y, 2, ROWS), f32),
            struct((LOCAL, 8, HS), f32),
        ),
        compiler_params=params(),
        cost_estimate=SMALL,
        name="norm",
    )(stats, scaled)
    sums = lax.all_to_all(sums, "seq", 0, 0, axis_index_groups=Y_GROUPS)
    trade = lambda x, i: lax.ppermute(x, "seq", swaps(Y * Z, i))
    queries_of = [q_mine] + [trade(q_mine, i) for i in (1, 2, 3)]
    coef = pl.pallas_call(
        coef_kernel,
        out_shape=struct((2, Y, LOCAL, ROWS, HS), f32),
        compiler_params=params(),
        cost_estimate=pl.CostEstimate(flops=1_000_000_000, bytes_accessed=1, transcendentals=0),
        name="coef",
    )(sums, gains)

    def attend(bulk, scales, *blocks):
        count = len(blocks)
        spare = 16 if count > 1 else 0
        return pl.pallas_call(
            functools.partial(attend_kernel, count),
            out_shape=(struct((PART + spare, HS), bf16),) * count
            + (struct((Y, LOCAL, 256, HS), bf16),) * (count > 1),
            scratch_shapes=[pltpu.VMEM((Y, ROWS, count * ROWS), f32)] * 2,
            compiler_params=params(),
            cost_estimate=pl.CostEstimate(
                flops=402_653_184 * count, bytes_accessed=4_000_000, transcendentals=262_144 * count
            ),
            name="attend" + "".join(map(str, blocks)),
        )(bulk, scales, *[queries_of[i] for i in blocks])

    part2, part3, normed = attend(bulk, coef, 2, 3)
    bulk, part2, part3 = lax.optimization_barrier((bulk, part2, part3))
    (part1,) = attend(bulk, normed, 1)
    bulk, part1 = lax.optimization_barrier((bulk, part1))
    (part0,) = attend(bulk, normed, 0)
    last = trade(part1, 1)
    sums, stats = pl.pallas_call(
        three_kernel,
        out_shape=(struct((LOCAL, 2, HS, ROWS), f32), struct((LOCAL, 2, 8, ROWS), f32)),
        compiler_params=params(),
        cost_estimate=SMALL,
        name="three",
    )(part0, trade(part2, 2), trade(part3, 3))
    out, tangent = pl.pallas_call(
        merge_kernel,
        out_shape=(struct((ROWS * LOCAL, HS), bf16),) * 2,
        scratch_shapes=[wide(2)],
        compiler_params=params(),
        cost_estimate=SMALL,
        name="merge",
    )(sums, stats, last)
    shape = queries.shape
    return (out.reshape(shape), tangent.reshape(shape))


def solution(mesh):
    token = P("seq", "dp", None)
    return jax.shard_map(
        shards,
        mesh=mesh,
        in_specs=(token,) * 6 + (P("dp"), P("dp")),
        out_specs=(token, token),
        check_vma=False,
    )
```

```python
import functools
import math

import jax
import jax.numpy as jnp
from jax import lax
from jax.experimental import pallas as pl
from jax.experimental.pallas import tpu as pltpu
from jax.sharding import PartitionSpec as P

HS = 128
HEADS = 32
FEATURES = HEADS * HS
EPSILON = 1e-06
FACTOR = HS**-0.5
LOG2E = math.log2(math.e)

Y, Z, DP = 8, 4, 16
ROWS = 128
LOCAL = 2
PART = 528

Z_GROUPS = [[y * Z + z for z in range(Z)] for y in range(Y)]
Y_GROUPS = [[y * Z + z for y in range(Y)] for z in range(Z)]

VMEM_LIMIT = 40 * 1024 * 1024
VMEM_WHOLE = 60 * 1024 * 1024
SMALL = pl.CostEstimate(flops=1, bytes_accessed=1, transcendentals=0)


def params(limit=VMEM_LIMIT):
    return pltpu.CompilerParams(vmem_limit_bytes=limit)


def swaps(size, bits):
    return [(i, i ^ bits) for i in range(size)]


def loader(refs, raw, wide, sems):
    loads = [pltpu.make_async_copy(ref, raw.at[i], sems.at[i]) for i, ref in enumerate(refs)]
    for load in loads:
        load.start()

    def heads(i):
        loads[i].wait()
        wide[i] = raw[i].astype(jnp.float32)
        return [wide[i, pl.ds(h, ROWS, stride=LOCAL), :] for h in range(LOCAL)]

    return heads


def stats_kernel(q, k, tq, tk, gain_q, gain_k, stat_out, scaled_out, raw, wide, gains, sems):
    gain_loads = [
        pltpu.make_async_copy(ref, gains.at[i], sems.at[4 + i])
        for i, ref in enumerate((gain_q, gain_k))
    ]
    for load in gain_loads:
        load.start()
    heads = loader((q, tq, k, tk), raw, wide, sems)
    pairs = [heads(i) for i in range(4)]
    for load in gain_loads:
        load.wait()
    rows = []
    for i in (0, 1):
        primal, tangent = pairs[2 * i], pairs[2 * i + 1]
        for other in (primal, tangent):
            product = primal[0] * other[0] + primal[1] * other[1]
            rows.append(jnp.sum(product.T, axis=0, keepdims=True))
        if i == 0:
            for h in range(LOCAL):
                scaled_out[0, h, 0:ROWS] = gains[0, h : h + 1] * primal[h]
                scaled_out[1, h, 0:ROWS] = gains[0, h : h + 1] * tangent[h]
                tail = jnp.broadcast_to(gains[1, h : h + 1], (8, HS))
                scaled_out[0, h, ROWS:] = tail
                scaled_out[1, h, ROWS:] = tail
    stat_out[...] = jnp.broadcast_to(jnp.concatenate(rows, axis=0)[None], stat_out.shape)


def split_three(x):
    high = x.astype(jnp.bfloat16).astype(jnp.float32)
    rest = x - high
    middle = rest.astype(jnp.bfloat16).astype(jnp.float32)
    return [high, middle, rest - middle]


def bulk_kernel(k, tk, v, tv, out, raw, wide, packed, sems):
    heads = loader((k, tk, v, tv), raw, wide, sems)
    pairs = [heads(i) for i in range(4)]
    for i, pair in enumerate(pairs):
        for h, block in enumerate(pair):
            block = block if i < 2 else block.T
            packed[h, i * 128 : (i + 1) * 128] = block.astype(jnp.bfloat16)
    send = pltpu.make_async_copy(packed, out, sems.at[4])
    send.start()
    send.wait()


def inverse_and_cross(squares, crosses):
    inverse = lax.rsqrt(squares * (1.0 / FEATURES) + EPSILON)
    cross = inverse * inverse * inverse * (crosses * (1.0 / FEATURES))
    return [jnp.broadcast_to(row, (ROWS, ROWS)).T for row in (inverse, cross)]


def norm_kernel(parts, scaled, q_out, key_out, gain_out):
    bf16 = jnp.bfloat16
    stats = jnp.sum(parts[...], axis=0)
    inverse, cross = inverse_and_cross(stats[0:1], stats[1:2])
    for h in range(LOCAL):
        primal, tangent = scaled[0, h, 0:ROWS], scaled[1, h, 0:ROWS]
        gain_out[h] = scaled[0, h, ROWS:]
        q_out[h, 0:128] = (primal * inverse).astype(bf16)
        q_out[h, 128:256] = (tangent * inverse - primal * cross).astype(bf16)
    key_out[...] = jnp.broadcast_to(stats[2:4][None], key_out.shape)


def stack_rows(rows, cols):
    index = lax.broadcasted_iota(jnp.int32, (16, cols), 0)
    tile = jnp.zeros((16, cols), jnp.float32)
    for i, row in enumerate(rows):
        tile = jnp.where(index == i, row, tile)
    return tile.astype(jnp.bfloat16)


def coef_kernel(sums, gains, coef):
    for y in range(Y):
        inverse, cross = inverse_and_cross(sums[y, 0:1], sums[y, 1:2])
        for h in range(LOCAL):
            coef[0, y, h] = inverse * gains[h, 0:1]
            coef[1, y, h] = cross * gains[h, 0:1]


def attend_kernel(count, bulk, normed, *refs):
    f32, bf16 = jnp.float32, jnp.bfloat16
    queries, outs, (s_ref, t_ref) = refs[:count], refs[count : 2 * count], refs[-2:]
    if count > 1:
        coef, normed = normed, refs[2 * count]
    nt = (((1,), (1,)), ((), ()))
    cols = count * ROWS

    rows = []
    for h in range(LOCAL):
        if count > 1:
            for y in range(Y):
                key = bulk[y, h, 0:128].astype(f32)
                tan_key = bulk[y, h, 128:256].astype(f32)
                normed[y, h, 0:128] = (key * coef[0, y, h]).astype(bf16)
                normed[y, h, 128:256] = (tan_key * coef[0, y, h] - key * coef[1, y, h]).astype(bf16)
        query = jnp.concatenate([q[h, 0:128] for q in queries], axis=0)
        tan_query = jnp.concatenate([q[h, 128:256] for q in queries], axis=0)
        both = jnp.concatenate([tan_query, query], axis=1)
        high = None
        for start in range(0, Y, 4):
            key = jnp.concatenate([normed[y, h, 0:128] for y in range(start, start + 4)], axis=0)
            score = lax.dot_general(key, query, nt, preferred_element_type=f32)
            for i, y in enumerate(range(start, start + 4)):
                scaled = score[i * 128 : (i + 1) * 128] * (FACTOR * LOG2E)
                s_ref[y] = scaled
                block_high = jnp.max(scaled.reshape(16, 8, cols), axis=0)
                high = block_high if high is None else jnp.maximum(high, block_high)
        high = jnp.max(high, axis=0, keepdims=True)
        total = jnp.zeros((8, cols), f32)
        cross = jnp.zeros((8, cols), f32)
        out = jnp.zeros((HS, cols), f32)
        tangent = jnp.zeros((HS, cols), f32)
        for start in range(0, Y, 2):
            pair = range(start, start + 2)
            keys = jnp.concatenate(
                [
                    jnp.concatenate([normed[y, h, first : first + 128] for y in pair], axis=0)
                    for first in (0, 128)
                ],
                axis=1,
            )
            tan = lax.dot_general(keys, both, nt, preferred_element_type=f32)
            lows = []
            for i, y in enumerate(pair):
                scaled = s_ref[y]
                weight = jnp.exp2(scaled - high)
                tan_score = tan[i * 128 : (i + 1) * 128] * FACTOR
                s_ref[y] = weight
                t_ref[y] = tan_score
                total = total + jnp.sum(weight.reshape(16, 8, cols), axis=0)
                cross = cross + jnp.sum((weight * tan_score).reshape(16, 8, cols), axis=0)
                lows.append(weight.astype(bf16))
            values = jnp.concatenate(
                [
                    jnp.concatenate([bulk[y, h, first : first + 128] for y in pair], axis=1)
                    for first in (256, 384)
                ],
                axis=0,
            )
            sums = jnp.dot(values, jnp.concatenate(lows, axis=0), preferred_element_type=f32)
            out = out + sums[0:128]
            tangent = tangent + sums[128:256]
        total = jnp.sum(total, axis=0, keepdims=True)
        inverse = 1.0 / total
        mean = jnp.sum(cross, axis=0, keepdims=True) * inverse
        for start in range(0, Y, 2):
            pair = range(start, start + 2)
            tan_lows = [(s_ref[y] * (t_ref[y] - mean)).astype(bf16) for y in pair]
            tangent = tangent + jnp.dot(
                jnp.concatenate([bulk[y, h, 256:384] for y in pair], axis=1),
                jnp.concatenate(tan_lows, axis=0),
                preferred_element_type=f32,
            )
        out = (out * inverse).astype(bf16)
        tangent = (tangent * inverse).astype(bf16)
        rows += split_three(high + jnp.log2(total)) + split_three(mean)
        for i, ref in enumerate(outs):
            lanes = slice(i * ROWS, (i + 1) * ROWS)
            ref[h * 256 : h * 256 + 128] = out[:, lanes]
            ref[h * 256 + 128 : h * 256 + 256] = tangent[:, lanes]
    stats = stack_rows(rows, cols)
    for i, ref in enumerate(outs):
        ref[512:PART] = stats[:, i * ROWS : (i + 1) * ROWS]
        if ref.shape[0] > PART:
            ref[PART:] = jnp.zeros((ref.shape[0] - PART, HS), bf16)


def statistics(part, h):
    rows = part[512:528].astype(jnp.float32)[6 * h : 6 * h + 6]
    return rows[0:1] + rows[1:2] + rows[2:3], rows[3:4] + rows[4:5] + rows[5:6]


def three_kernel(p0, p2, p3, sum_out, stat_out):
    f32 = jnp.float32
    for h in range(LOCAL):
        logs, means = zip(*[statistics(part, h) for part in (p0, p2, p3)])
        top = jnp.maximum(jnp.maximum(logs[0], logs[1]), logs[2])
        weights = [jnp.exp2(x - top) for x in logs]
        total = weights[0] + weights[1] + weights[2]
        inverse = 1.0 / total
        weights = [w * inverse for w in weights]
        mean = sum(w * m for w, m in zip(weights, means))
        out = jnp.zeros((HS, ROWS), f32)
        tangent = jnp.zeros((HS, ROWS), f32)
        for part, weight, own_mean in zip((p0, p2, p3), weights, means):
            piece = part[h * 256 : h * 256 + 128].astype(f32)
            out = out + weight * piece
            tangent = tangent + weight * part[h * 256 + 128 : h * 256 + 256].astype(f32)
            tangent = tangent + (weight * (own_mean - mean)) * piece
        sum_out[h, 0], sum_out[h, 1] = out, tangent
        stat_out[h, 0] = jnp.broadcast_to(top + jnp.log2(total), (8, ROWS))
        stat_out[h, 1] = jnp.broadcast_to(mean, (8, ROWS))


def merge_kernel(sums, stats, last, out_ref, tan_ref, wide):
    f32, bf16 = jnp.float32, jnp.bfloat16
    for h in range(LOCAL):
        log, mean = stats[h, 0, 0:1], stats[h, 1, 0:1]
        last_log, last_mean = statistics(last, h)
        top = jnp.maximum(log, last_log)
        weight, last_weight = jnp.exp2(log - top), jnp.exp2(last_log - top)
        inverse = 1.0 / (weight + last_weight)
        weight, last_weight = weight * inverse, last_weight * inverse
        piece = last[h * 256 : h * 256 + 128].astype(f32)
        tan_piece = last[h * 256 + 128 : h * 256 + 256].astype(f32)
        out = weight * sums[h, 0] + last_weight * piece
        tangent = weight * sums[h, 1] + last_weight * tan_piece
        tangent = tangent + (weight * last_weight * (mean - last_mean)) * (sums[h, 0] - piece)
        wide[0, pl.ds(h, ROWS, stride=LOCAL), :] = out.T
        wide[1, pl.ds(h, ROWS, stride=LOCAL), :] = tangent.T
    out_ref[...] = wide[0].astype(bf16)
    tan_ref[...] = wide[1].astype(bf16)


def shards(queries, keys, values, tan_queries, tan_keys, tan_values, gain_q, gain_k):
    f32, bf16 = jnp.float32, jnp.bfloat16
    flat = lambda x: x.reshape(ROWS * LOCAL, HS)
    q, k, v = flat(queries), flat(keys), flat(values)
    tq, tk, tv = flat(tan_queries), flat(tan_keys), flat(tan_values)
    raw = lambda n: pltpu.VMEM((n, ROWS * LOCAL, HS), bf16)
    wide = lambda n: pltpu.VMEM((n, ROWS * LOCAL, HS), f32)
    hbm = pl.BlockSpec(memory_space=pltpu.HBM)
    vmem = pl.BlockSpec(memory_space=pltpu.VMEM)
    struct = jax.ShapeDtypeStruct
    block = (Y, LOCAL, 256, HS)

    stats, scaled = pl.pallas_call(
        stats_kernel,
        out_shape=(struct((DP, 4, ROWS), f32), struct((2, LOCAL, ROWS + 8, HS), f32)),
        in_specs=[hbm] * 6,
        out_specs=(vmem, vmem),
        scratch_shapes=[
            raw(4),
            wide(4),
            pltpu.VMEM((2, LOCAL, HS), f32),
            pltpu.SemaphoreType.DMA((6,)),
        ],
        compiler_params=params(VMEM_WHOLE),
        cost_estimate=SMALL,
        name="stats",
    )(q, k, tq, tk, gain_q.reshape(LOCAL, HS), gain_k.reshape(LOCAL, HS))
    bulk = pl.pallas_call(
        bulk_kernel,
        out_shape=struct((LOCAL, 512, HS), bf16),
        in_specs=[hbm] * 4,
        out_specs=hbm,
        scratch_shapes=[
            raw(4),
            wide(4),
            pltpu.VMEM((LOCAL, 512, HS), bf16),
            pltpu.SemaphoreType.DMA((5,)),
        ],
        compiler_params=params(VMEM_WHOLE),
        cost_estimate=SMALL,
        name="bulk",
    )(k, tk, v, tv)
    bulk = lax.all_gather(bulk, "seq", axis_index_groups=Y_GROUPS)
    stats = lax.all_to_all(stats, "dp", 0, 0)
    q_mine, sums, gains = pl.pallas_call(
        norm_kernel,
        out_shape=(
            struct((LOCAL, 256, HS), bf16),
            struct((Y, 2, ROWS), f32),
            struct((LOCAL, 8, HS), f32),
        ),
        compiler_params=params(),
        cost_estimate=SMALL,
        name="norm",
    )(stats, scaled)
    sums = lax.all_to_all(sums, "seq", 0, 0, axis_index_groups=Y_GROUPS)
    trade = lambda x, i: lax.ppermute(x, "seq", swaps(Y * Z, i))
    queries_of = [q_mine] + [trade(q_mine, i) for i in (1, 2, 3)]
    coef = pl.pallas_call(
        coef_kernel,
        out_shape=struct((2, Y, LOCAL, ROWS, HS), f32),
        compiler_params=params(),
        cost_estimate=pl.CostEstimate(flops=1_000_000_000, bytes_accessed=1, transcendentals=0),
        name="coef",
    )(sums, gains)

    def attend(bulk, scales, *blocks):
        count = len(blocks)
        spare = 16 if count > 1 else 0
        return pl.pallas_call(
            functools.partial(attend_kernel, count),
            out_shape=(struct((PART + spare, HS), bf16),) * count
            + (struct((Y, LOCAL, 256, HS), bf16),) * (count > 1),
            scratch_shapes=[pltpu.VMEM((Y, ROWS, count * ROWS), f32)] * 2,
            compiler_params=params(),
            cost_estimate=pl.CostEstimate(
                flops=402_653_184 * count, bytes_accessed=4_000_000, transcendentals=262_144 * count
            ),
            name="attend" + "".join(map(str, blocks)),
        )(bulk, scales, *[queries_of[i] for i in blocks])

    part2, part3, normed = attend(bulk, coef, 2, 3)
    bulk, part2, part3 = lax.optimization_barrier((bulk, part2, part3))
    (part1,) = attend(bulk, normed, 1)
    bulk, part1 = lax.optimization_barrier((bulk, part1))
    (part0,) = attend(bulk, normed, 0)
    last = trade(part1, 1)
    sums, stats = pl.pallas_call(
        three_kernel,
        out_shape=(struct((LOCAL, 2, HS, ROWS), f32), struct((LOCAL, 2, 8, ROWS), f32)),
        compiler_params=params(),
        cost_estimate=SMALL,
        name="three",
    )(part0, trade(part2, 2), trade(part3, 3))
    out, tangent = pl.pallas_call(
        merge_kernel,
        out_shape=(struct((ROWS * LOCAL, HS), bf16),) * 2,
        scratch_shapes=[wide(2)],
        compiler_params=params(),
        cost_estimate=SMALL,
        name="merge",
    )(sums, stats, last)
    shape = queries.shape
    return (out.reshape(shape), tangent.reshape(shape))


def solution(mesh):
    token = P("seq", "dp", None)
    return jax.shard_map(
        shards,
        mesh=mesh,
        in_specs=(token,) * 6 + (P("dp"), P("dp")),
        out_specs=(token, token),
        check_vma=False,
    )
```
